512 devices in a mesh: head: 2 (over core), ctx: 256 (over y, x, z).
Axes of the slice: x: 4, y: 8, z: 8, core: 2. Of those that a mesh axis runs over, the one named last changes fastest.
Arguments:
- queries: bfloat16 [32768, 4096], P('ctx', 'head'), may hold values from -4.5 to 4.5
- key_rows: bfloat16 [32768, 512], P('ctx'), may hold values from -4.5 to 4.5
- value_rows: bfloat16 [32768, 512], P('ctx'), may hold values from -4.5 to 4.5
- out_grad: bfloat16 [32768, 4096], P('ctx', 'head'), may hold values from -6 to 6
- partner_keep: int32 [256, 3], P('ctx'), may hold values 0 or 1
Outputs:
- attended: bfloat16 [32768, 4096], P('ctx', 'head')
- query_grad: bfloat16 [32768, 4096], P('ctx', 'head')
- key_grad: bfloat16 [32768, 512], P('ctx')
- value_grad: bfloat16 [32768, 512], P('ctx')
The draws below stay inside these ranges and needn't reach their ends.
All inputs are finite; a program needn't handle non-finite values. No bound on the sum of `partner_keep` on one device may be relied on, other than what follows from the above.
Results may differ from the reference program's by a relative error of at most 0.0093.
The reference program's roundings to bfloat16 on the way count: a program that leaves them out, or rounds other values in their place, can miss the bound.
Values may be sent and summed in bfloat16 or wider, within the bound.
No kernel may reach another device: no remote copies, remote signals or barrier semaphores. Data moves between devices by JAX's collectives and lax.ppermute only.
A program may use at most 64 MiB of HBM per device.

```python
import jax
import jax.numpy as jnp
from jax import lax

KVH = 4
HD = 128
TOK_DEV = 128
POOL = 32
LEVELS = 3
GROUP = 8
QD = 4096
KVD = 512
NBLK = 256
TOKENS = 32768
LMS = 1024


def pooled_common(group_key):
    common = jax.random.normal(group_key, (LMS, KVD), jnp.float32)
    return jnp.repeat(common, POOL, axis=0)


def draw_queries(key, part):
    base_key = jax.random.fold_in(key, 11)
    values = jnp.clip(jax.random.normal(base_key, (TOKENS, QD), jnp.float32), -4.5, 4.5)
    return values.astype(jnp.bfloat16)


def draw_key_rows(key, part):
    base_key = jax.random.fold_in(key, 23)
    common = pooled_common(jax.random.fold_in(key, 29))
    values = 0.6 * jax.random.normal(base_key, (TOKENS, KVD), jnp.float32) + 0.8 * common
    values = jnp.clip(values, -4.5, 4.5)
    return values.astype(jnp.bfloat16)


def draw_value_rows(key, part):
    base_key = jax.random.fold_in(key, 37)
    common = pooled_common(jax.random.fold_in(key, 41))
    values = 0.6 * jax.random.normal(base_key, (TOKENS, KVD), jnp.float32) + 0.8 * common
    return jnp.clip(values, -4.5, 4.5).astype(jnp.bfloat16)


def place_ends(values, rng, least, largest):
    place = [jax.random.randint(jax.random.fold_in(rng, axis), (), 0, length) for axis, length in enumerate(values.shape)]
    widest = values.shape.index(max(values.shape))
    next_to = place[:widest] + [(place[widest] + 1) % values.shape[widest]] + place[widest + 1:]
    return values.at[tuple(place)].set(least).at[tuple(next_to)].set(largest)


def levels(key, dims, pieces, smallest, largest):
    level, own = 1.0, jax.random.fold_in(key, 6)
    for axis_at, parts in pieces:
        draws = jnp.exp(jax.random.uniform(jax.random.fold_in(own, axis_at), (parts,), jnp.float32, smallest / len(pieces), largest / len(pieces)))
        level = level * jnp.repeat(draws, dims[axis_at] // parts).reshape([-1 if axis == axis_at else 1 for axis in range(len(dims))])
    return level


def gaussian(key, extent, width, bound, cuts=(), kind=jnp.bfloat16):
    values = jax.random.normal(key, extent, jnp.float32) * width
    if len(cuts) > 0:
        values = levels(key, extent, cuts, -0.22, 0.18) * values
    return jnp.clip(values, min=-bound, max=bound).astype(kind)


def setup_inputs(seed: int = 0) -> dict:
    keys = jax.random.split(jax.random.key(seed), 6)
    queries = draw_queries(jax.random.fold_in(keys[5], 71), 0)
    key_rows = draw_key_rows(jax.random.fold_in(keys[5], 71), 0)
    value_rows = draw_value_rows(jax.random.fold_in(keys[5], 71), 0)
    out_grad = gaussian(keys[3], (TOKENS, QD), 1.0, 6.0, ((0, 256), (1, 2)))
    partner_keep = place_ends((jax.random.randint(keys[4], (NBLK, LEVELS), 0, 4) < 3).astype(jnp.int32), jax.random.fold_in(keys[4], 1), 0, 1)
    return {"queries": queries, "key_rows": key_rows, "value_rows": value_rows, "out_grad": out_grad, "partner_keep": partner_keep}


def masked_scores(query_rows, key_block, live_mask, score_scale):
    raw_scores = jnp.dot(query_rows, key_block.T, preferred_element_type=jnp.float32)
    return jnp.where(live_mask, raw_scores * score_scale, -jnp.inf)


def head_terms(query_rows, dout_rows, local_keys, local_values, land_keys, land_values, local_mask, land_mask, score_scale):
    local_scores = masked_scores(query_rows, local_keys, local_mask, score_scale)
    land_scores = masked_scores(query_rows, land_keys, land_mask, score_scale)
    peak_rows = jnp.maximum(jnp.max(local_scores, axis=1), jnp.max(land_scores, axis=1))
    totals = jnp.sum(jnp.exp(local_scores - peak_rows[:, None]), axis=1) + jnp.sum(jnp.exp(land_scores - peak_rows[:, None]), axis=1)
    log_sums = peak_rows + jnp.log(totals)
    local_soft = jnp.exp(local_scores - log_sums[:, None])
    land_soft = jnp.exp(land_scores - log_sums[:, None])
    local_half = local_soft.astype(jnp.bfloat16)
    land_half = land_soft.astype(jnp.bfloat16)
    output_rows = (jnp.dot(local_half, local_values, preferred_element_type=jnp.float32) + jnp.dot(land_half, land_values, preferred_element_type=jnp.float32)).astype(jnp.bfloat16)
    delta_rows = jnp.sum(dout_rows.astype(jnp.float32) * output_rows.astype(jnp.float32), axis=1)
    local_dsoft = jnp.dot(dout_rows, local_values.T, preferred_element_type=jnp.float32)
    land_dsoft = jnp.dot(dout_rows, land_values.T, preferred_element_type=jnp.float32)
    local_dscore = (local_soft * (local_dsoft - delta_rows[:, None])).astype(jnp.bfloat16)
    land_dscore = (land_soft * (land_dsoft - delta_rows[:, None])).astype(jnp.bfloat16)
    query_part = (score_scale * (jnp.dot(local_dscore, local_keys, preferred_element_type=jnp.float32) + jnp.dot(land_dscore, land_keys, preferred_element_type=jnp.float32))).astype(jnp.bfloat16)
    key_part = score_scale * jnp.dot(local_dscore.T, query_rows, preferred_element_type=jnp.float32)
    value_part = jnp.dot(local_half.T, dout_rows, preferred_element_type=jnp.float32)
    return output_rows, query_part, key_part, value_part


def add_rows(accum, new_rows, first_row):
    current = lax.dynamic_slice_in_dim(accum, first_row, new_rows.shape[0], 0)
    return lax.dynamic_update_slice_in_dim(accum, current + new_rows, first_row, 0)


def reference(queries, key_rows, value_rows, out_grad, partner_keep):
    score_scale = HD ** -0.5
    land_keys = key_rows.astype(jnp.float32).reshape(LMS, POOL, KVD).mean(axis=1).astype(jnp.bfloat16)
    land_values = value_rows.astype(jnp.float32).reshape(LMS, POOL, KVD).mean(axis=1).astype(jnp.bfloat16)
    land_index = jnp.arange(LMS, dtype=jnp.int32) // (TOK_DEV // POOL)
    row_pos = jnp.arange(TOK_DEV * GROUP, dtype=jnp.int32) // GROUP
    columns = jnp.arange(TOK_DEV * (1 + LEVELS), dtype=jnp.int32)

    def one_block(carried, block_id):
        key_acc, value_acc = carried
        first = block_id * TOK_DEV
        query_blk = lax.dynamic_slice_in_dim(queries, first, TOK_DEV, 0)
        dout_blk = lax.dynamic_slice_in_dim(out_grad, first, TOK_DEV, 0)
        key_parts = [lax.dynamic_slice_in_dim(key_rows, first, TOK_DEV, 0)]
        value_parts = [lax.dynamic_slice_in_dim(value_rows, first, TOK_DEV, 0)]
        live_parts = [jnp.ones((TOK_DEV,), jnp.bool_)]
        partner_ids = []
        for level_index in range(LEVELS):
            distance = NBLK // 2 ** (level_index + 1)
            partner = jnp.bitwise_xor(block_id, distance).astype(jnp.int32)
            partner_ids.append(partner)
            key_parts.append(lax.dynamic_slice_in_dim(key_rows, partner * TOK_DEV, TOK_DEV, 0))
            value_parts.append(lax.dynamic_slice_in_dim(value_rows, partner * TOK_DEV, TOK_DEV, 0))
            wanted = jnp.logical_and(partner < block_id, partner_keep[block_id, level_index] == 1)
            live_parts.append(jnp.broadcast_to(wanted, (TOK_DEV,)))
        local_keys = jnp.concatenate(key_parts, axis=0)
        local_values = jnp.concatenate(value_parts, axis=0)
        live_cols = jnp.concatenate(live_parts)
        local_mask = jnp.where(columns[None, :] < TOK_DEV, columns[None, :] <= row_pos[:, None], live_cols[None, :])
        land_mask = (land_index < block_id)[None, :]
        outputs = []
        query_grads = []
        key_cols = []
        value_cols = []
        for head_index in range(KVH):
            query_rows = query_blk[:, head_index * GROUP * HD:(head_index + 1) * GROUP * HD].reshape(TOK_DEV * GROUP, HD)
            dout_rows = dout_blk[:, head_index * GROUP * HD:(head_index + 1) * GROUP * HD].reshape(TOK_DEV * GROUP, HD)
            low_col = head_index * HD
            result = head_terms(query_rows, dout_rows, local_keys[:, low_col:low_col + HD], local_values[:, low_col:low_col + HD], land_keys[:, low_col:low_col + HD], land_values[:, low_col:low_col + HD], local_mask, land_mask, score_scale)
            outputs.append(result[0].reshape(TOK_DEV, GROUP * HD))
            query_grads.append(result[1].reshape(TOK_DEV, GROUP * HD))
            key_cols.append(result[2])
            value_cols.append(result[3])
        key_local = jnp.concatenate(key_cols, axis=1)
        value_local = jnp.concatenate(value_cols, axis=1)
        key_acc = add_rows(key_acc, key_local[:TOK_DEV], first)
        value_acc = add_rows(value_acc, value_local[:TOK_DEV], first)
        for level_index in range(LEVELS):
            row_lower = TOK_DEV * (level_index + 1)
            key_acc = add_rows(key_acc, key_local[row_lower:row_lower + TOK_DEV], partner_ids[level_index] * TOK_DEV)
            value_acc = add_rows(value_acc, value_local[row_lower:row_lower + TOK_DEV], partner_ids[level_index] * TOK_DEV)
        return (key_acc, value_acc), (jnp.concatenate(outputs, axis=1), jnp.concatenate(query_grads, axis=1))

    start_acc = (jnp.zeros((TOKENS, KVD), jnp.float32), jnp.zeros((TOKENS, KVD), jnp.float32))
    finals, stacked = lax.scan(one_block, start_acc, jnp.arange(NBLK, dtype=jnp.int32))
    attended = stacked[0].reshape(TOKENS, QD)
    query_grad = stacked[1].reshape(TOKENS, QD)
    return attended, query_grad, finals[0].astype(jnp.bfloat16), finals[1].astype(jnp.bfloat16)
```

```python
import functools

import jax
import jax.numpy as jnp
from jax import lax
from jax.experimental import pallas as pl
from jax.experimental.pallas import tpu as pltpu
from jax.sharding import PartitionSpec as P

HD = 128
POOL = 32
LEVELS = 3
TOK = 128
CHUNK = 256
BIG = -1e30
SCALE = HD**-0.5
LOG2E = 1.4426950408889634
F32 = jnp.float32
BF16 = jnp.bfloat16
NT = (((1,), (1,)), ((), ()))
NN = (((1,), (0,)), ((), ()))
TN = (((0,), (0,)), ((), ()))

FIRST = [
    [(2 * yk + yb) * 32 + x * 8 + 2 * zk + zb for yk in range(4) for zk in range(4)]
    for yb in range(2)
    for x in range(4)
    for zb in range(2)
]
SECOND = [
    [(2 * yk + yb) * 32 + x * 8 + 2 * zk + zb for yb in range(2) for x in range(4) for zb in range(2)]
    for yk in range(4)
    for zk in range(4)
]


def mul(a, b, dims):
    return lax.dot_general(a, b, dims, preferred_element_type=F32)


def pool_kernel(key_ref, value_ref, kv_ref, land_ref):
    col = pl.multiple_of(lax.axis_index("head") * 256, 256)
    parts = []
    for ref, low in ((key_ref, 0), (value_ref, 256)):
        rows = ref[:, pl.ds(col, 256)]
        kv_ref[:, low : low + 256] = rows
        wide = rows.astype(F32)
        parts.append(
            jnp.concatenate(
                [jnp.sum(wide[j * POOL : (j + 1) * POOL], axis=0, keepdims=True) for j in range(TOK // POOL)],
                axis=0,
            )
            * (1.0 / POOL)
        )
    land = jnp.concatenate(parts, axis=1)
    copies = land_ref.shape[0] // land.shape[0]
    land_ref[...] = jnp.concatenate([land] * copies, axis=0).astype(BF16)


def pool(key_rows, value_rows):
    return pl.pallas_call(
        pool_kernel,
        out_shape=(
            jax.ShapeDtypeStruct((TOK, 512), BF16),
            jax.ShapeDtypeStruct((4 * len(FIRST[0]), 512), BF16),
        ),
    )(key_rows, value_rows)


def land_block(row):
    first = (row >> 2) & 15
    second = row >> 6
    y = ((first >> 2) << 1) | (second >> 3)
    x = (second >> 1) & 3
    z = ((first & 3) << 1) | (second & 1)
    return y * 32 + x * 8 + z


def attend_kernel(
    ctx_count,
    keep_ref,
    q_ref,
    do_ref,
    own_ref,
    p0_ref,
    p1_ref,
    p2_ref,
    land_ref,
    att_ref,
    dq_ref,
    own_grad_ref,
    g0_ref,
    g1_ref,
    g2_ref,
    keys,
    values,
    work,
    dk,
    dv,
):
    step = pl.program_id(0)
    block = lax.axis_index("ctx")
    partners = (p0_ref, p1_ref, p2_ref)
    n_keys = keys.shape[0]
    n_local = TOK * (1 + LEVELS)

    @pl.when(step == 0)
    def _():
        row = lax.broadcasted_iota(jnp.int32, (TOK, TOK), 0)
        col = lax.broadcasted_iota(jnp.int32, (TOK, TOK), 1)
        keys[:TOK, HD:] = jnp.where(row > col, BIG, 0.0).astype(BF16)
        for level in range(LEVELS):
            distance = ctx_count // 2 ** (level + 1)
            wanted = jnp.logical_and((block // distance) % 2 == 1, keep_ref[0, level] == 1)
            bias = jnp.where(wanted, 0.0, BIG)
            keys[TOK * (level + 1) : TOK * (level + 2), HD:] = jnp.full((TOK, HD), bias, F32).astype(BF16)
        row = lax.broadcasted_iota(jnp.int32, (n_keys - n_local, HD), 0)
        keys[n_local:, HD:] = jnp.where(land_block(row) < block, 0.0, BIG).astype(BF16)

    for head in range(2):

        @pl.when(step == 4 * head)
        def _():
            k_cols = slice(head * HD, (head + 1) * HD)
            v_cols = slice(256 + head * HD, 256 + (head + 1) * HD)
            for number, ref in enumerate((own_ref,) + partners):
                keys[number * TOK : (number + 1) * TOK, :HD] = ref[:, k_cols]
                values[number * TOK : (number + 1) * TOK, :] = ref[:, v_cols]
            keys[n_local:, :HD] = land_ref[:, k_cols]
            values[n_local:, :] = land_ref[:, v_cols]
            dk[...] = jnp.zeros_like(dk)
            dv[...] = jnp.zeros_like(dv)

    q = jnp.concatenate([q_ref[:, :HD], q_ref[:, HD:]], axis=0)
    do = jnp.concatenate([do_ref[:, :HD], do_ref[:, HD:]], axis=0)
    rows = q.shape[0]
    token = lax.broadcasted_iota(jnp.int32, (rows, HD), 0) & (TOK - 1)
    pick = jnp.where(token == lax.broadcasted_iota(jnp.int32, (rows, HD), 1), 1.0, 0.0)
    q_pick = jnp.concatenate([q, pick.astype(BF16)], axis=1)
    chunks = [slice(low, low + CHUNK) for low in range(0, n_keys, CHUNK)]

    peak = None
    for chunk in chunks:
        score = mul(q_pick, keys[chunk, :], NT) * (SCALE * LOG2E)
        work[:, chunk] = score
        for low in range(0, CHUNK, 128):
            piece = score[:, low : low + 128]
            peak = piece if peak is None else jnp.maximum(peak, piece)
    peak = jnp.max(peak, axis=1, keepdims=True)
    total = None
    for chunk in chunks:
        prob = jnp.exp2(work[:, chunk] - peak)
        work[:, chunk] = prob
        for low in range(0, CHUNK, 128):
            piece = prob[:, low : low + 128]
            total = piece if total is None else total + piece
    inverse = 1.0 / jnp.sum(total, axis=1, keepdims=True)
    out = None
    for number, chunk in enumerate(chunks):
        soft = work[:, chunk] * inverse
        work[:, chunk] = soft
        half = soft.astype(BF16)
        term = mul(half, values[chunk, :], NN)
        out = term if out is None else out + term
        if number < n_local // CHUNK:
            dv[chunk, :] += mul(half, do, TN)
    out = out.astype(BF16)
    att_ref[:, :HD] = out[:TOK]
    att_ref[:, HD:] = out[TOK:]
    delta = jnp.sum(do.astype(F32) * out.astype(F32), axis=1, keepdims=True)
    dq = None
    for number, chunk in enumerate(chunks):
        dsoft = mul(do, values[chunk, :], NT)
        dscore = (work[:, chunk] * (dsoft - delta)).astype(BF16)
        term = mul(dscore, keys[chunk, :HD], NN)
        dq = term if dq is None else dq + term
        if number < n_local // CHUNK:
            dk[chunk, :] += mul(dscore, q, TN)
    dq = (SCALE * dq).astype(BF16)
    dq_ref[:, :HD] = dq[:TOK]
    dq_ref[:, HD:] = dq[TOK:]

    for head in range(2):

        @pl.when(step == 4 * head + 3)
        def _():
            for source, factor, low in ((dk, SCALE, head * HD), (dv, 1.0, 256 + head * HD)):
                own_grad_ref[:, low : low + HD] = source[:TOK, :] * factor
                for level, ref in enumerate((g0_ref, g1_ref, g2_ref)):
                    part = source[TOK * (level + 1) : TOK * (level + 2), :] * factor
                    ref[:, low : low + HD] = part.astype(BF16)


def attend(ctx_count, partner_keep, queries, out_grad, own, partners, land):
    n_keys = TOK * (1 + LEVELS) + land.shape[0]
    wide = pl.BlockSpec((TOK, 256), lambda i: (0, i))
    whole = pl.BlockSpec((TOK, 512), lambda i: (0, 0))
    return pl.pallas_call(
        functools.partial(attend_kernel, ctx_count),
        grid=(8,),
        in_specs=[
            pl.BlockSpec(memory_space=pltpu.SMEM),
            wide,
            wide,
            whole,
            whole,
            whole,
            whole,
            pl.BlockSpec(land.shape, lambda i: (0, 0)),
        ],
        out_specs=[wide, wide, whole, whole, whole, whole],
        out_shape=[
            jax.ShapeDtypeStruct((TOK, 2048), BF16),
            jax.ShapeDtypeStruct((TOK, 2048), BF16),
            jax.ShapeDtypeStruct((TOK, 512), F32),
        ]
        + [jax.ShapeDtypeStruct((TOK, 512), BF16)] * LEVELS,
        scratch_shapes=[
            pltpu.VMEM((n_keys, 2 * HD), BF16),
            pltpu.VMEM((n_keys, HD), BF16),
            pltpu.VMEM((256, n_keys), F32),
            pltpu.VMEM((TOK * (1 + LEVELS), HD), F32),
            pltpu.VMEM((TOK * (1 + LEVELS), HD), F32),
        ],
        compiler_params=pltpu.CompilerParams(vmem_limit_bytes=32 * 2**20),
    )(partner_keep, queries, out_grad, own, *partners, land)


def total_kernel(own_ref, r0_ref, r1_ref, r2_ref, sum_ref):
    total = own_ref[...]
    for ref in (r0_ref, r1_ref, r2_ref):
        total = total + ref[...].astype(F32)
    sum_ref[...] = total.astype(BF16)


def exchange(rows, groups):
    return lax.all_to_all(rows, "ctx", 0, 0, axis_index_groups=groups, tiled=True)


def local(queries, key_rows, value_rows, out_grad, partner_keep):
    ctx_count = lax.axis_size("ctx")
    own, land = pool(key_rows, value_rows)
    pairs = []
    for level in range(LEVELS):
        distance = ctx_count // 2 ** (level + 1)
        pairs.append([(b, b + distance) for b in range(ctx_count) if b // distance % 2 == 0])
    partners = [lax.ppermute(own, "ctx", pair) for pair in pairs]
    land = exchange(land, FIRST)
    land = jnp.broadcast_to(land[None], (len(SECOND[0]),) + land.shape)
    land = exchange(land, SECOND).reshape(-1, 512)
    att, dq, own_grad, *sent = attend(ctx_count, partner_keep, queries, out_grad, own, partners, land)
    back = [
        lax.ppermute(part, "ctx", [(later, earlier) for earlier, later in pair]) for part, pair in zip(sent, pairs)
    ]
    total = pl.pallas_call(total_kernel, out_shape=jax.ShapeDtypeStruct((TOK, 512), BF16))(own_grad, *back)
    both = lax.all_gather(total, "head", axis=0)
    key_grad = jnp.concatenate([both[0, :, :256], both[1, :, :256]], axis=1)
    value_grad = jnp.concatenate([both[0, :, 256:], both[1, :, 256:]], axis=1)
    return att, dq, key_grad, value_grad


def solution(mesh):
    placed = (P("ctx", "head"), P("ctx", None), P("ctx", None), P("ctx", "head"), P("ctx", None))
    return jax.shard_map(
        local,
        mesh=mesh,
        in_specs=placed,
        out_specs=(P("ctx", "head"), P("ctx", "head"), P("ctx", None), P("ctx", None)),
        check_vma=False,
    )
```

```python
import functools

import jax
import jax.numpy as jnp
from jax import lax
from jax.experimental import pallas as pl
from jax.experimental.pallas import tpu as pltpu
from jax.sharding import PartitionSpec as P

HD = 128
POOL = 32
LEVELS = 3
TOK = 128
CHUNK = 256
BIG = -1e30
SCALE = HD**-0.5
LOG2E = 1.4426950408889634
F32 = jnp.float32
BF16 = jnp.bfloat16
NT = (((1,), (1,)), ((), ()))
NN = (((1,), (0,)), ((), ()))
TN = (((0,), (0,)), ((), ()))

FIRST = [[y * 32 + x * 8 + z for y in range(8) for z in range(8)] for x in range(4)]
SECOND = [[y * 32 + x * 8 + z for x in range(4)] for y in range(8) for z in range(8)]


def mul(a, b, dims):
    return lax.dot_general(a, b, dims, preferred_element_type=F32)


def pool_kernel(key_ref, value_ref, kv_ref, land_ref):
    col = pl.multiple_of(lax.axis_index("head") * 256, 256)
    parts = []
    for ref, low in ((key_ref, 0), (value_ref, 256)):
        rows = ref[:, pl.ds(col, 256)]
        kv_ref[:, low : low + 256] = rows
        wide = rows.astype(F32)
        parts.append(
            jnp.concatenate(
                [jnp.sum(wide[j * POOL : (j + 1) * POOL], axis=0, keepdims=True) for j in range(TOK // POOL)],
                axis=0,
            )
            * (1.0 / POOL)
        )
    land = jnp.concatenate(parts, axis=1)
    land_ref[...] = jnp.broadcast_to(land.astype(BF16)[None], land_ref.shape)


def pool(key_rows, value_rows):
    return pl.pallas_call(
        pool_kernel,
        out_shape=(
            jax.ShapeDtypeStruct((TOK, 512), BF16),
            jax.ShapeDtypeStruct((len(FIRST[0]), TOK // POOL, 512), BF16),
        ),
        compiler_params=pltpu.CompilerParams(vmem_limit_bytes=4 * 2**20),
    )(key_rows, value_rows)


def land_block(row):
    first = (row >> 2) & 63
    y, x, z = first >> 3, row >> 8, first & 7
    return y * 32 + x * 8 + z


def token_pick(rows):
    token = lax.broadcasted_iota(jnp.int32, (rows, HD), 0) & (TOK - 1)
    return jnp.where(token == lax.broadcasted_iota(jnp.int32, (rows, HD), 1), 1.0, 0.0).astype(BF16)


def land_bias(shape, axis):
    row = lax.broadcasted_iota(jnp.int32, shape, axis)
    return jnp.where(land_block(row) < lax.axis_index("ctx"), 0.0, BIG).astype(BF16)


def two_heads(ref, low):
    both = ref[:, pl.ds(low, 2 * HD)]
    return jnp.concatenate([both[:, :HD], both[:, HD:]], axis=0)


def side_by_side(rows):
    return jnp.concatenate([rows[:TOK], rows[TOK:]], axis=1)


def add(total, term):
    return term if total is None else total + term


def fold(combine, total, wide):
    for low in range(0, wide.shape[1], 128):
        piece = wide[:, low : low + 128]
        total = piece if total is None else combine(total, piece)
    return total


def cut(low, high):
    return [slice(at, at + CHUNK) for at in range(low, high, CHUNK)]


def attend_kernel(
    ctx_count,
    keep_ref,
    q_ref,
    do_ref,
    own_ref,
    p0_ref,
    p1_ref,
    p2_ref,
    land_ref,
    att_ref,
    dq_ref,
    stats_ref,
    own_grad_ref,
    g0_ref,
    g1_ref,
    g2_ref,
    keys,
    keys_t,
    values,
    values_t,
    work,
    dk,
    dv,
):
    block = lax.axis_index("ctx")
    n_keys = values.shape[0]
    n_local = TOK * (1 + LEVELS)

    row = lax.broadcasted_iota(jnp.int32, (TOK, TOK), 0)
    col = lax.broadcasted_iota(jnp.int32, (TOK, TOK), 1)
    keys_t[HD:, :TOK] = jnp.where(col > row, BIG, 0.0).astype(BF16)
    for level in range(LEVELS):
        distance = ctx_count // 2 ** (level + 1)
        wanted = jnp.logical_and((block // distance) % 2 == 1, keep_ref[0, level] == 1)
        bias = jnp.where(wanted, 0.0, BIG)
        keys_t[HD:, TOK * (level + 1) : TOK * (level + 2)] = jnp.full((HD, TOK), bias, F32).astype(BF16)
    keys_t[HD:, n_local:] = land_bias((HD, n_keys - n_local), 1)
    stats_ref[...] = jnp.zeros_like(stats_ref)
    pick = token_pick(2 * TOK)
    lane = lax.broadcasted_iota(jnp.int32, (2 * TOK, 128), 1)

    for head in range(2):
        k_cols = slice(head * HD, (head + 1) * HD)
        v_cols = slice(256 + head * HD, 256 + (head + 1) * HD)
        for number, ref in enumerate((own_ref, p0_ref, p1_ref, p2_ref)):
            rows = slice(number * TOK, (number + 1) * TOK)
            k_rows = ref[:, k_cols]
            v_rows = ref[:, v_cols]
            keys[rows, :] = k_rows
            keys_t[:HD, rows] = k_rows.T
            values[rows, :] = v_rows
            values_t[:, rows] = v_rows.T
        keys_t[:HD, n_local:] = land_ref[:, k_cols].T
        values[n_local:, :] = land_ref[:, v_cols]
        dk[...] = jnp.zeros_like(dk)
        dv[...] = jnp.zeros_like(dv)

        @pl.loop(0, 4)
        def _(step):
            number = head * 4 + step
            low = pl.multiple_of(number * 2 * HD, 2 * HD)
            q = two_heads(q_ref, low)
            do = two_heads(do_ref, low)
            q_pick = jnp.concatenate([q, pick], axis=1)

            peak = None
            for chunk in cut(0, n_keys):
                score = mul(q_pick, keys_t[:, chunk], NN) * (SCALE * LOG2E)
                work[:, chunk] = score
                peak = fold(jnp.maximum, peak, score)
            peak = jnp.max(peak, axis=1, keepdims=True)
            total = out = None
            for chunk in cut(0, n_keys):
                prob = jnp.exp2(work[:, chunk] - peak)
                if chunk.start < n_local:
                    work[:, chunk] = prob
                total = fold(jnp.add, total, prob)
                out = add(out, mul(prob.astype(BF16), values[chunk, :], NN))
            total = jnp.sum(total, axis=1, keepdims=True)
            inverse = 1.0 / total
            out = (out * inverse).astype(BF16)
            att_ref[:, pl.ds(low, 2 * HD)] = side_by_side(out)
            delta = jnp.sum(do.astype(F32) * out.astype(F32), axis=1, keepdims=True)
            stats = jnp.where(lane == 2 * number, peak + jnp.log2(total), stats_ref[...])
            stats_ref[...] = jnp.where(lane == 2 * number + 1, delta, stats)
            dq = None
            for chunk in cut(0, n_local):
                soft = work[:, chunk] * inverse
                dv[chunk, :] += mul(soft.astype(BF16), do, TN)
                dsoft = mul(do, values_t[:, chunk], NN)
                dscore = (soft * (dsoft - delta)).astype(BF16)
                dq = add(dq, mul(dscore, keys[chunk, :], NN))
                dk[chunk, :] += mul(dscore, q, TN)
            dq_ref[:, pl.ds(low, 2 * HD)] = side_by_side(dq)

        for source, factor, low in ((dk, SCALE, head * HD), (dv, 1.0, 256 + head * HD)):
            own_grad_ref[:, low : low + HD] = source[:TOK, :] * factor
            for level, ref in enumerate((g0_ref, g1_ref, g2_ref)):
                part = source[TOK * (level + 1) : TOK * (level + 2), :] * factor
                ref[:, low : low + HD] = part.astype(BF16)


def attend(ctx_count, partner_keep, queries, out_grad, own, partners, land):
    n_local = TOK * (1 + LEVELS)
    n_keys = n_local + land.shape[0]
    vmem = pl.BlockSpec(memory_space=pltpu.VMEM)
    return pl.pallas_call(
        functools.partial(attend_kernel, ctx_count),
        in_specs=[pl.BlockSpec(memory_space=pltpu.SMEM)] + [vmem] * 7,
        out_specs=[vmem] * 7,
        out_shape=[
            jax.ShapeDtypeStruct((TOK, 2048), BF16),
            jax.ShapeDtypeStruct((TOK, 2048), F32),
            jax.ShapeDtypeStruct((2 * TOK, 128), F32),
            jax.ShapeDtypeStruct((TOK, 512), F32),
        ]
        + [jax.ShapeDtypeStruct((TOK, 512), BF16)] * LEVELS,
        scratch_shapes=[
            pltpu.VMEM((n_local, HD), BF16),
            pltpu.VMEM((2 * HD, n_keys), BF16),
            pltpu.VMEM((n_keys, HD), BF16),
            pltpu.VMEM((HD, n_local), BF16),
            pltpu.VMEM((2 * TOK, n_keys), F32),
            pltpu.VMEM((n_local, HD), F32),
            pltpu.VMEM((n_local, HD), F32),
        ],
        compiler_params=pltpu.CompilerParams(vmem_limit_bytes=24 * 2**20),
        cost_estimate=pl.CostEstimate(flops=5 * 10**9, bytes_accessed=4 * 2**20, transcendentals=4 * 10**6),
    )(partner_keep, queries, out_grad, own, *partners, land)


def land_kernel(q_ref, do_ref, land_ref, part_ref, stats_ref, dq_ref, keys, keys_t, values_t):
    n_keys = keys.shape[0]
    keys_t[HD:, :] = land_bias((HD, n_keys), 1)
    pick = token_pick(2 * TOK)
    lane = lax.broadcasted_iota(jnp.int32, (2 * TOK, 128), 1)
    for head in range(2):
        keys[...] = land_ref[:, head * HD : (head + 1) * HD]
        keys_t[:HD, :] = keys[...].T
        values_t[...] = land_ref[:, 256 + head * HD : 256 + (head + 1) * HD].T

        @pl.loop(0, 4)
        def _(step):
            number = head * 4 + step
            low = pl.multiple_of(number * 2 * HD, 2 * HD)
            q = two_heads(q_ref, low)
            do = two_heads(do_ref, low)
            q_pick = jnp.concatenate([q, pick], axis=1)
            stats = stats_ref[...]
            log_sum = jnp.sum(jnp.where(lane == 2 * number, stats, 0.0), axis=1, keepdims=True)
            delta = jnp.sum(jnp.where(lane == 2 * number + 1, stats, 0.0), axis=1, keepdims=True)
            dq = two_heads(part_ref, low)
            for chunk in cut(0, n_keys):
                score = mul(q_pick, keys_t[:, chunk], NN) * (SCALE * LOG2E)
                soft = jnp.exp2(score - log_sum)
                dsoft = mul(do, values_t[:, chunk], NN)
                dscore = (soft * (dsoft - delta)).astype(BF16)
                dq = dq + mul(dscore, keys[chunk, :], NN)
            dq_ref[:, pl.ds(low, 2 * HD)] = side_by_side((SCALE * dq).astype(BF16))


def land_backward(queries, out_grad, land, part, stats):
    vmem = pl.BlockSpec(memory_space=pltpu.VMEM)
    n_keys = land.shape[0]
    return pl.pallas_call(
        land_kernel,
        in_specs=[vmem] * 5,
        out_specs=vmem,
        out_shape=jax.ShapeDtypeStruct((TOK, 2048), BF16),
        scratch_shapes=[
            pltpu.VMEM((n_keys, HD), BF16),
            pltpu.VMEM((2 * HD, n_keys), BF16),
            pltpu.VMEM((HD, n_keys), BF16),
        ],
        compiler_params=pltpu.CompilerParams(vmem_limit_bytes=24 * 2**20),
        cost_estimate=pl.CostEstimate(flops=4 * 10**9, bytes_accessed=4 * 2**20, transcendentals=2 * 10**6),
    )(queries, out_grad, land, part, stats)


def total_kernel(own_ref, r0_ref, r1_ref, r2_ref, sum_ref):
    total = own_ref[...]
    for ref in (r0_ref, r1_ref, r2_ref):
        total = total + ref[...].astype(F32)
    sum_ref[...] = total.astype(BF16)


def exchange(rows, groups):
    return lax.all_to_all(rows, "ctx", 0, 0, axis_index_groups=groups, tiled=True)


def local(queries, key_rows, value_rows, out_grad, partner_keep):
    ctx_count = lax.axis_size("ctx")
    own, land = pool(key_rows, value_rows)
    pairs = []
    for level in range(LEVELS):
        distance = ctx_count // 2 ** (level + 1)
        pairs.append([(b, b + distance) for b in range(ctx_count) if b // distance % 2 == 0])
    partners = [lax.ppermute(own, "ctx", pair) for pair in pairs]
    land = exchange(land, FIRST)
    land, partners = lax.optimization_barrier((land, partners))
    land = jnp.broadcast_to(land.reshape(1, -1, 512), (len(SECOND[0]), land.shape[0] * land.shape[1], 512))
    land = exchange(land, SECOND).reshape(-1, 512)
    att, part, stats, own_grad, *sent = attend(ctx_count, partner_keep, queries, out_grad, own, partners, land)
    dq = land_backward(queries, out_grad, land, part, stats)
    back = [
        lax.ppermute(part, "ctx", [(later, earlier) for earlier, later in pair]) for part, pair in zip(sent, pairs)
    ]
    total = pl.pallas_call(
        total_kernel,
        out_shape=jax.ShapeDtypeStruct((TOK, 512), BF16),
        compiler_params=pltpu.CompilerParams(vmem_limit_bytes=4 * 2**20),
    )(own_grad, *back)
    both = lax.all_gather(total, "head", axis=0)
    key_grad = jnp.concatenate([both[0, :, :256], both[1, :, :256]], axis=1)
    value_grad = jnp.concatenate([both[0, :, 256:], both[1, :, 256:]], axis=1)
    return att, dq, key_grad, value_grad


def solution(mesh):
    placed = (P("ctx", "head"), P("ctx", None), P("ctx", None), P("ctx", "head"), P("ctx", None))
    return jax.shard_map(
        local,
        mesh=mesh,
        in_specs=placed,
        out_specs=(P("ctx", "head"), P("ctx", "head"), P("ctx", None), P("ctx", None)),
        check_vma=False,
    )
```
